32 devices in a mesh: modes: 4 (over y, x), atoms: 8 (over z, core).
Axes of the slice: x: 2, y: 2, z: 4, core: 2. Of those that a mesh axis runs over, the one named last changes fastest.
Arguments:
- left_modes: bfloat16 [3, 8192, 3072], P(None, 'atoms', 'modes'), may hold values from -6 to 6
- right_panel: bfloat16 [3, 8192, 256], P(None, 'atoms', 'modes'), may hold values from -6 to 6
- force_blocks: float32 [3, 3, 16, 8192], P(None, None, None, 'atoms'), may hold values from -0.875 to 0.875
- bond_vectors: float32 [3, 16, 8192], P(None, None, 'atoms'), may hold values from -1 to 1
- neighbours: int32 [16, 8192], P(None, 'atoms'), may hold values from 0 to 8191, as said below
- counts: int32 [8192], P('atoms'), may hold values from 1 to 16
- left_bins: int32 [3072], P(('modes', 'atoms')), may hold values from 1 to 32
- right_bins: int32 [256], replicated, may hold values from 1 to 32
Outputs:
- diffusivity: float32 [3072], P(('modes', 'atoms'))
The draws below stay inside these ranges and needn't reach their ends.
Inputs may be any that keep to these rules, and one draw needn't show every extreme that they name: neighbours[k, a] = (a + s) modulo 8192 with 1 <= |s| <= 256; some entry has |s| = 256.
All inputs are finite; a program needn't handle non-finite values.
Results may differ from the reference program's by a relative error of at most 0.00058.
Values may be sent and summed in bfloat16 or wider, within the bound.
A program may use at most 128 MiB of HBM per device.

```python
import math
import jax
import jax.numpy as jnp
from jax import lax

PANEL = 256
K = 16
NBINS = 32
HALO = 256
ATOMS = 8192
LEFT = 3072


def draw_neighbours(key, part):
    key_size, key_sign, key_far = jax.random.split(jax.random.fold_in(key, 7), 3)
    distance = jax.random.randint(key_size, (K, ATOMS), 1, HALO + 1)
    direction_sign = jax.random.randint(key_sign, (K, ATOMS), 0, 2) * 2 - 1
    offsets = distance * direction_sign
    far_atoms = jax.random.randint(key_far, (2,), 0, ATOMS)
    offsets = offsets.at[0, far_atoms[0]].set(HALO)
    offsets = offsets.at[0, far_atoms[1]].set(-HALO)
    atom_ids = lax.broadcasted_iota(jnp.int32, (K, ATOMS), 1)
    return jnp.mod(atom_ids + offsets, ATOMS).astype(jnp.int32)


def set_ends(drawn, own_key, low, largest):
    spot = [jax.random.randint(jax.random.fold_in(own_key, axis), (), 0, length) for axis, length in enumerate(drawn.shape)]
    main_axis = drawn.shape.index(max(drawn.shape))
    beside = spot[:main_axis] + [(spot[main_axis] + 1) % drawn.shape[main_axis]] + spot[main_axis + 1:]
    return drawn.at[tuple(spot)].set(low).at[tuple(beside)].set(largest)


def with_spikes(array, own_key, source, target, parts, factor):
    owner, partner = [(jnp.arange(array.shape[position]) // (array.shape[position] // parts)).reshape([-1 if axis == position else 1 for axis in range(array.ndim)]) for position in (source, target)]
    chosen = jax.random.permutation(own_key, parts)[partner]
    strong = (owner == chosen) | (owner == (partner + parts // 2) % parts)
    return jnp.where(strong, factor * array, array)


def levels(rng, extent, pieces, low, top_value):
    def one(axis_at, blocks):
        steps = jax.random.uniform(jax.random.fold_in(jax.random.fold_in(rng, 6), axis_at), (blocks,), jnp.float32, low / len(pieces), top_value / len(pieces))
        return jnp.repeat(jnp.exp(steps), extent[axis_at] // blocks).reshape((-1,) + (1,) * (len(extent) - axis_at - 1))

    loudness = one(*pieces[0])
    for cut in pieces[1:]:
        loudness = loudness * one(*cut)
    return loudness


def bell_draw(own_key, dims, spread, most, cuts=(), kind=jnp.bfloat16):
    array = jax.random.normal(own_key, dims, jnp.float32) * spread
    if len(cuts) > 0:
        array = levels(own_key, dims, cuts, -0.22, 0.18) * array
    return jnp.clip(array, min=-most, max=most).astype(kind)


def noise_with(stream_key, extent, spread, most, cuts, heavy, kind=jnp.bfloat16):
    drawn = spread * jax.random.normal(stream_key, extent, jnp.float32)
    if cuts:
        drawn = drawn * levels(stream_key, extent, cuts, -0.22, 0.18)
    return jnp.clip(with_spikes(drawn, jax.random.fold_in(stream_key, 3), *heavy), -most, most).astype(kind)


def setup_inputs(seed: int = 0) -> dict:
    key_of = jax.random.split(jax.random.key(seed), 9)
    return {
        "left_modes": noise_with(key_of[0], (3, ATOMS, LEFT), 1.0, 6.0, ((1, 8), (2, 4)), (1, 2, 8, 2.0)),
        "right_panel": bell_draw(key_of[1], (3, ATOMS, PANEL), 1.0, 6.0, ((1, 8), (2, 4))),
        "force_blocks": bell_draw(key_of[2], (3, 3, K, ATOMS), (3 * K) ** -0.5, 0.875, ((3, 8),), jnp.float32),
        "bond_vectors": jnp.clip(jax.random.uniform(key_of[3], (3, K, ATOMS), jnp.float32, -1.0, 1.0) * levels(key_of[3], (3, K, ATOMS), ((2, 8),), -0.4, 0.0), -1.0, 1.0),
        "neighbours": draw_neighbours(jax.random.fold_in(key_of[8], 71), 0),
        "counts": set_ends(jax.random.randint(key_of[5], (ATOMS,), 1, K + 1), jax.random.fold_in(key_of[5], 1), 1, K).astype(jnp.int32),
        "left_bins": set_ends(jax.random.randint(key_of[6], (LEFT,), 1, NBINS + 1), jax.random.fold_in(key_of[6], 1), 1, NBINS).astype(jnp.int32),
        "right_bins": set_ends(jax.random.randint(key_of[7], (PANEL,), 1, NBINS + 1), jax.random.fold_in(key_of[7], 1), 1, NBINS).astype(jnp.int32),
    }


omega_step = 0.05
gamma = 0.1


def operator_blocks(force_blocks, bond_vectors, counts):
    slot_ids = lax.broadcasted_iota(jnp.int32, bond_vectors.shape[1:], 0)
    live_slot = (slot_ids < counts[None, :]).astype(jnp.float32)
    scaled = bond_vectors * live_slot[None]
    return (scaled[:, None, None, :, :] * force_blocks[None]).astype(jnp.bfloat16)


def reference(left_modes, right_panel, force_blocks, bond_vectors, neighbours, counts, left_bins, right_bins):
    blocks = operator_blocks(force_blocks, bond_vectors, counts)
    block_width = math.gcd(ATOMS, 256)
    starts = jnp.arange(ATOMS // block_width, dtype=jnp.int32) * block_width

    def one_block(start_row):
        near_index = lax.dynamic_slice_in_dim(neighbours, start_row, block_width, 1)
        nearby = right_panel[:, near_index, :].astype(jnp.float32)
        coefficient = lax.dynamic_slice_in_dim(blocks, start_row, block_width, 4).astype(jnp.float32)
        return jnp.einsum('xcdkb,dkbj->xcbj', coefficient, nearby).astype(jnp.bfloat16)

    stacked = lax.map(one_block, starts)
    flux_all = jnp.moveaxis(stacked, 0, 2).reshape(3, 3 * ATOMS, PANEL)
    left_flat = left_modes.reshape(3 * ATOMS, LEFT)
    squares = jnp.zeros((LEFT, PANEL), jnp.float32)
    for direction in range(3):
        coupling = lax.dot_general(left_flat, flux_all[direction], (((0,), (0,)), ((), ())), preferred_element_type=jnp.float32)
        squares = squares + coupling * coupling
    omega_left = omega_step * left_bins.astype(jnp.float32)
    omega_right = omega_step * right_bins.astype(jnp.float32)
    freq_gap = omega_left[:, None] - omega_right[None, :]
    weight = gamma * gamma / (freq_gap * freq_gap + gamma * gamma)
    weight = weight * (omega_left[:, None] + omega_right[None, :]) ** 2 / (4.0 * omega_left[:, None] * omega_right[None, :])
    return 4.0 * jnp.sum(weight * squares, axis=1) / (ATOMS * PANEL)
```

```python
import functools

import jax
import jax.numpy as jnp
from jax import lax
from jax.experimental import pallas as pl
from jax.experimental.pallas import tpu as pltpu
from jax.sharding import PartitionSpec as P

omega_step = 0.05
gamma = 0.1
F32, BF16 = jnp.float32, jnp.bfloat16
MESH = pl.DeviceIdType.MESH
NT = (((1,), (1,)), ((), ()))


def kernel(
    nm, na,
    rt, left, force, bond, nbr, counts, lbins, rbins, out,
    rx, lv, mat, lt, nrow, flux, cacc, csend, crecv, zsend, zrecv, own,
    g_send, g_recv, h_send, h_recv, c_send, c_recv, z_send, z_recv, l_sem, o_sem,
):
    slots, atoms = nbr.shape
    cols = rt.shape[1]
    halo = atoms // 4
    blocks = atoms // halo
    win = 3 * halo
    sub = lt.shape[1]
    per = lt.shape[2] // slots
    wide = lt.shape[2]
    rows = lbins.shape[0]
    nz = na // 2
    panel = cols * nm
    nl = left.shape[2]
    total_atoms = atoms * na
    m = lax.axis_index("modes")
    a = lax.axis_index("atoms")
    core = lax.rem(a, 2)
    z = a // 2
    up, down = lax.rem(a + 1, na), lax.rem(a + na - 1, na)
    sibling = a + 1 - 2 * core

    def at(mode, atom):
        return {"modes": mode, "atoms": atom}

    barrier = pltpu.get_barrier_semaphore()
    friends = [at(lax.rem(m + p, nm), a) for p in range(1, nm)]
    friends += [at(m, up), at(m, down)]
    friends += [at(m, lax.rem(a + 2 * q, na)) for q in range(1, nz)]
    for friend in friends:
        pl.semaphore_signal(barrier, inc=1, device_id=friend, device_id_type=MESH)
    lcopies = [
        pltpu.make_async_copy(left.at[c], lv.at[pl.ds(c * atoms, atoms)], l_sem.at[c])
        for c in range(3)
    ]
    for copy in lcopies:
        copy.start()
    pl.semaphore_wait(barrier, len(friends))

    my_rows = pl.ds(pl.multiple_of(m * cols, cols), cols)
    pieces = ((0, halo), (atoms - halo, halo), (halo, atoms - 2 * halo))

    def gather(p, i):
        lane, count = pieces[i]
        return pltpu.make_async_remote_copy(
            src_ref=rt.at[:, :, pl.ds(lane, count)],
            dst_ref=rx.at[:, my_rows, pl.ds(halo + lane, count)],
            send_sem=g_send.at[p - 1, i],
            recv_sem=g_recv.at[p - 1, i],
            device_id=at(lax.rem(m + p, nm), a),
            device_id_type=MESH,
        )

    def edge(p, i):
        lane = pieces[i][0]
        who = lax.rem(m + nm - p, nm)
        its_rows = pl.ds(pl.multiple_of(who * cols, cols), cols)
        src = rt.at[:, :, pl.ds(lane, halo)] if p == 0 else rx.at[:, its_rows, pl.ds(halo + lane, halo)]
        return pltpu.make_async_remote_copy(
            src_ref=src,
            dst_ref=rx.at[:, its_rows, pl.ds(halo + atoms if i == 0 else 0, halo)],
            send_sem=h_send.at[p, i],
            recv_sem=h_recv.at[p, i],
            device_id=at(m, down if i == 0 else up),
            device_id_type=MESH,
        )

    own_copy = pltpu.make_async_copy(rt, rx.at[:, my_rows, pl.ds(halo, atoms)], o_sem)
    own_copy.start()
    for i in range(3):
        for p in range(1, nm):
            gather(p, i).start()
        if i < 2:
            edge(0, i).start()

    lane_id = lax.broadcasted_iota(jnp.int32, (sub, wide), 1)
    row_id = lax.broadcasted_iota(jnp.int32, (sub, wide), 0)
    diag = lax.rem(row_id, per) == lax.rem(lane_id, per)
    k_row = lax.broadcasted_iota(jnp.int32, (128, wide), 0)
    k_lane = lax.broadcasted_iota(jnp.int32, (128, wide), 1) // per
    groups_128 = 128 // slots

    def build(u, carry):
        t = u // (halo // sub)
        r0 = lax.rem(u, halo // sub) * sub
        lanes = pl.ds(pl.multiple_of(u * sub, sub), sub)
        slot_ids = lax.broadcasted_iota(jnp.int32, (slots, sub), 0)
        live = (slot_ids < counts[:, lanes]).astype(F32)
        parts = []
        for x in range(3):
            scaled = bond[x, :, lanes] * live
            for cd in range(9):
                parts.append(scaled * force[cd, :, lanes])
        rel = nbr[:, lanes] - (a * atoms + t * halo - halo)
        rel = jnp.where(rel < 0, rel + total_atoms, rel)
        rel = jnp.where(rel >= total_atoms, rel - total_atoms, rel)
        parts.append((rel // 16).astype(F32))
        parts.append(lax.rem(rel, 16).astype(F32))
        while len(parts) % groups_128:
            parts.append(jnp.zeros((slots, sub), F32))
        spread = []
        for s in range(len(parts) // groups_128):
            block = jnp.concatenate(parts[s * groups_128:(s + 1) * groups_128], axis=0)
            spread.append(block.T.astype(BF16))

        def expand(i):
            chosen = (k_row == lax.rem(i, groups_128) * slots + k_lane).astype(F32).astype(BF16)
            return lax.dot_general(
                spread[i // groups_128], chosen, (((1,), (0,)), ((), ())),
                preferred_element_type=F32,
            )

        for i in range(27):
            lt[i] = jnp.where(diag, expand(i), 0.0).astype(BF16)
        index = jnp.where(diag, 16.0 * expand(27) + expand(28), 0.0)
        nrow[...] = jnp.sum(index.reshape(sub // per, per, wide), axis=1)

        def group(g, carry2):
            row = nrow[pl.ds(g, 1), :]
            here = pl.ds(pl.multiple_of(g * per, per), per)
            there = pl.ds(pl.multiple_of(r0 + g * per, per), per)
            lhs = lt[:, here, :].reshape(27 * per, wide)
            for n in range(3):
                b = lax.broadcasted_iota(jnp.int32, (halo, wide), 0).astype(F32) + float(n * halo)
                hot = (b == row).astype(F32).astype(BF16)
                res = lax.dot_general(lhs, hot, NT, preferred_element_type=F32).astype(BF16)
                res = res.reshape(9, 3, per, halo)
                for d in range(3):
                    mat[t, :, there, pl.ds(d * win + n * halo, halo)] = res[:, d]
            return carry2

        lax.fori_loop(0, sub // per, group, 0)
        return carry

    units = atoms // sub
    first = units // 2
    lax.fori_loop(0, first, build, 0)
    for i in range(2):
        for p in range(1, nm):
            gather(p, i).wait_recv()
            edge(p, i).start()
    lax.fori_loop(first, units, build, 0)
    own_copy.wait()
    for p in range(1, nm):
        gather(p, 2).wait_recv()
    for i in range(2):
        for p in range(nm):
            edge(p, i).wait_recv()
    for copy in lcopies:
        copy.wait()

    def cross(x):
        return pltpu.make_async_remote_copy(
            src_ref=csend.at[x], dst_ref=crecv.at[x],
            send_sem=c_send.at[x], recv_sem=c_recv.at[x],
            device_id=at(m, sibling), device_id_type=MESH,
        )

    def along(x, s):
        return pltpu.make_async_remote_copy(
            src_ref=zsend.at[x, s - 1], dst_ref=zrecv.at[x, s - 1],
            send_sem=z_send.at[x, s - 1], recv_sem=z_recv.at[x, s - 1],
            device_id=at(m, lax.rem(a + 2 * s, na)), device_id_type=MESH,
        )

    def owner_rows(o):
        return pl.ds(pl.multiple_of(o * rows, 8), rows)

    def forward(x):
        cross(x).wait_recv()
        for s in [*range(1, nz), 0]:
            q = lax.rem(z + s, nz)
            both = cacc[x % 2, owner_rows(2 * q + core), :] + crecv[x, q, :rows, :].astype(F32)
            if s:
                zsend[x, s - 1, :rows, :] = both.astype(BF16)
                along(x, s).start()
            else:
                own[x] = both

    for x in range(3):
        def one_flux(i, carry, x=x):
            c, t = i // blocks, lax.rem(i, blocks)
            acc = jnp.zeros((panel, halo), F32)
            for d in range(3):
                acc += lax.dot_general(
                    rx[d, :, pl.ds(pl.multiple_of(t * halo, halo), win)],
                    mat[t, 3 * x + c, :, pl.ds(d * win, win)],
                    NT, preferred_element_type=F32,
                )
            flux[:, pl.ds(pl.multiple_of(i * halo, halo), halo)] = acc.astype(BF16)
            return carry

        mid = blocks
        lax.fori_loop(0, mid, one_flux, 0)
        if x:
            forward(x - 1)
        lax.fori_loop(mid, 3 * blocks, one_flux, 0)

        def one_coupling(n, carry, x=x):
            lanes = pl.ds(pl.multiple_of(n * 256, 256), 256)
            part = jnp.dot(flux[...], lv[:, lanes], preferred_element_type=F32)
            cacc[x % 2, lanes, :] = part.T
            return carry

        lax.fori_loop(0, nl // 256, one_coupling, 0)
        for q in range(nz):
            csend[x, q, :rows, :] = cacc[x % 2, owner_rows(2 * q + 1 - core), :].astype(BF16)
        cross(x).start()
    forward(2)

    squares = jnp.zeros((rows, panel), F32)
    for x in range(3):
        total = own[x]
        for s in range(1, nz):
            along(x, s).wait_recv()
            total += zrecv[x, s - 1, :rows, :].astype(F32)
        squares += total * total
    omega_left = omega_step * lbins[...].astype(F32)
    omega_right = omega_step * rbins[...].astype(F32)
    gap = omega_left - omega_right
    weight = gamma * gamma / (gap * gap + gamma * gamma)
    both = omega_left + omega_right
    weight = weight * (both * both) / (4.0 * omega_left * omega_right)
    out[...] = 4.0 * jnp.sum(weight * squares, axis=1, keepdims=True) / (total_atoms * panel)

    for i in range(3):
        for p in range(1, nm):
            gather(p, i).wait_send()
    for i in range(2):
        for p in range(nm):
            edge(p, i).wait_send()
    for x in range(3):
        cross(x).wait_send()
        for s in range(1, nz):
            along(x, s).wait_send()


def per_device(
    nm, na,
    left_modes, right_panel, force_blocks, bond_vectors, neighbours, counts, left_bins, right_bins
):
    atoms, cols = right_panel.shape[1:]
    slots = neighbours.shape[0]
    nl = left_modes.shape[2]
    rows = left_bins.shape[0]
    panel = cols * nm
    halo = atoms // 4
    sub, wide = 128, 256
    nz = na // 2
    padded = -(-rows // 16) * 16
    vm = pl.BlockSpec(memory_space=pltpu.VMEM)
    hbm = pl.BlockSpec(memory_space=pl.ANY)
    dma = pltpu.SemaphoreType.DMA
    result = pl.pallas_call(
        functools.partial(kernel, nm, na),
        out_shape=jax.ShapeDtypeStruct((rows, 1), F32),
        in_specs=[hbm, hbm, vm, vm, vm, vm, vm, vm],
        out_specs=vm,
        scratch_shapes=[
            pltpu.VMEM((3, panel, atoms + 2 * halo), BF16),
            pltpu.VMEM((3 * atoms, nl), BF16),
            pltpu.VMEM((atoms // halo, 9, halo, 9 * halo), BF16),
            pltpu.VMEM((27, sub, wide), BF16),
            pltpu.VMEM((sub * slots // wide, wide), F32),
            pltpu.VMEM((panel, 3 * atoms), BF16),
            pltpu.VMEM((2, nl, panel), F32),
            pltpu.VMEM((3, nz, padded, panel), BF16),
            pltpu.VMEM((3, nz, padded, panel), BF16),
            pltpu.VMEM((3, nz - 1, padded, panel), BF16),
            pltpu.VMEM((3, nz - 1, padded, panel), BF16),
            pltpu.VMEM((3, rows, panel), F32),
            dma((nm - 1, 3)), dma((nm - 1, 3)),
            dma((nm, 2)), dma((nm, 2)),
            dma((3,)), dma((3,)),
            dma((3, nz - 1)), dma((3, nz - 1)),
            dma((3,)), dma,
        ],
        compiler_params=pltpu.CompilerParams(
            collective_id=0, has_side_effects=True, vmem_limit_bytes=60 * 2**20
        ),
    )(
        jnp.transpose(right_panel, (0, 2, 1)), left_modes,
        force_blocks.reshape(9, slots, atoms), bond_vectors, neighbours,
        counts[None, :], left_bins[:, None], right_bins[None, :],
    )
    return result[:, 0]


def solution(mesh):
    return jax.shard_map(
        functools.partial(per_device, mesh.shape["modes"], mesh.shape["atoms"]),
        mesh=mesh,
        in_specs=(
            P(None, "atoms", "modes"),
            P(None, "atoms", "modes"),
            P(None, None, None, "atoms"),
            P(None, None, "atoms"),
            P(None, "atoms"),
            P("atoms"),
            P(("modes", "atoms")),
            P(),
        ),
        out_specs=P(("modes", "atoms")),
        check_vma=False,
    )
```

```python
import functools

import jax
import jax.numpy as jnp
from jax import lax
from jax.experimental import pallas as pl
from jax.experimental.pallas import tpu as pltpu
from jax.sharding import PartitionSpec as P

omega_step = 0.05
gamma = 0.1
F32, BF16 = jnp.float32, jnp.bfloat16
MESH = pl.DeviceIdType.MESH
NT = (((1,), (1,)), ((), ()))


def kernel(
    nm, na,
    rt, left, force, bond, nbr, counts, lbins, rbins, out,
    rx, lv, mat, lt, flux, cacc, csend, crecv, zsend, zrecv, own,
    g_send, g_recv, h_send, h_recv, c_send, c_recv, z_send, z_recv, l_sem, o_sem,
):
    slots, atoms = nbr.shape
    cols = rt.shape[1]
    halo = atoms // 4
    blocks = atoms // halo
    win = 3 * halo
    sub = lt.shape[1]
    per = lt.shape[2] // slots
    wide = lt.shape[2]
    rows = lbins.shape[1]
    nz = na // 2
    panel = cols * nm
    nl = left.shape[2]
    total_atoms = atoms * na
    m = lax.axis_index("modes")
    a = lax.axis_index("atoms")
    core = lax.rem(a, 2)
    z = a // 2
    up, down = lax.rem(a + 1, na), lax.rem(a + na - 1, na)
    sibling = a + 1 - 2 * core

    def at(mode, atom):
        return {"modes": mode, "atoms": atom}

    barrier = pltpu.get_barrier_semaphore()
    friends = [at(lax.rem(m + p, nm), a) for p in range(1, nm)]
    friends += [at(m, up), at(m, down)]
    friends += [at(m, lax.rem(a + 2 * q, na)) for q in range(1, nz)]
    for friend in friends:
        pl.semaphore_signal(barrier, inc=1, device_id=friend, device_id_type=MESH)
    lcopies = [
        pltpu.make_async_copy(left.at[c], lv.at[pl.ds(c * atoms, atoms)], l_sem.at[c])
        for c in range(3)
    ]
    for copy in lcopies:
        copy.start()
    pl.semaphore_wait(barrier, len(friends))

    my_rows = pl.ds(pl.multiple_of(m * cols, cols), cols)
    pieces = ((0, halo), (atoms - halo, halo), (halo, atoms - 2 * halo))

    def gather(p, i):
        lane, count = pieces[i]
        return pltpu.make_async_remote_copy(
            src_ref=rt.at[:, :, pl.ds(lane, count)],
            dst_ref=rx.at[:, my_rows, pl.ds(halo + lane, count)],
            send_sem=g_send.at[p - 1, i],
            recv_sem=g_recv.at[p - 1, i],
            device_id=at(lax.rem(m + p, nm), a),
            device_id_type=MESH,
        )

    def edge(p, i):
        lane = pieces[i][0]
        who = lax.rem(m + nm - p, nm)
        its_rows = pl.ds(pl.multiple_of(who * cols, cols), cols)
        src = rt.at[:, :, pl.ds(lane, halo)] if p == 0 else rx.at[:, its_rows, pl.ds(halo + lane, halo)]
        return pltpu.make_async_remote_copy(
            src_ref=src,
            dst_ref=rx.at[:, its_rows, pl.ds(halo + atoms if i == 0 else 0, halo)],
            send_sem=h_send.at[p, i],
            recv_sem=h_recv.at[p, i],
            device_id=at(m, down if i == 0 else up),
            device_id_type=MESH,
        )

    own_copy = pltpu.make_async_copy(rt, rx.at[:, my_rows, pl.ds(halo, atoms)], o_sem)
    own_copy.start()
    for i in range(3):
        for p in range(1, nm):
            gather(p, i).start()
        if i < 2:
            edge(0, i).start()

    lane_id = lax.broadcasted_iota(jnp.int32, (sub, wide), 1)
    row_id = lax.broadcasted_iota(jnp.int32, (sub, wide), 0)
    diag = lax.rem(row_id, per) == lax.rem(lane_id, per)
    k_row = lax.broadcasted_iota(jnp.int32, (128, wide), 0)
    k_lane = lax.broadcasted_iota(jnp.int32, (128, wide), 1) // per
    groups_128 = 128 // slots
    b_lane = lax.broadcasted_iota(jnp.int32, (wide, halo), 1).astype(F32).astype(BF16)
    one, zero = jnp.ones((wide, halo), BF16), jnp.zeros((wide, halo), BF16)

    def build(u, carry):
        t = u // (halo // sub)
        r0 = lax.rem(u, halo // sub) * sub
        lanes = pl.ds(pl.multiple_of(u * sub, sub), sub)
        slot_ids = lax.broadcasted_iota(jnp.int32, (slots, sub), 0)
        live = (slot_ids < counts[:, lanes]).astype(F32)
        parts = []
        for x in range(3):
            scaled = bond[x, :, lanes] * live
            for cd in range(9):
                parts.append(scaled * force[cd, :, lanes])
        rel = nbr[:, lanes] - (a * atoms + t * halo - halo)
        rel = jnp.where(rel < 0, rel + total_atoms, rel)
        rel = jnp.where(rel >= total_atoms, rel - total_atoms, rel)
        parts.append((rel // 16).astype(F32))
        parts.append(lax.rem(rel, 16).astype(F32))
        while len(parts) % groups_128:
            parts.append(jnp.zeros((slots, sub), F32))
        spread = []
        for s in range(len(parts) // groups_128):
            block = jnp.concatenate(parts[s * groups_128:(s + 1) * groups_128], axis=0)
            spread.append(block.T.astype(BF16))

        def expand(i):
            chosen = (k_row == lax.rem(i, groups_128) * slots + k_lane).astype(F32).astype(BF16)
            return lax.dot_general(
                spread[i // groups_128], chosen, (((1,), (0,)), ((), ())),
                preferred_element_type=F32,
            )

        for i in range(27):
            lt[i] = jnp.where(diag, expand(i), 0.0).astype(BF16)
        index = jnp.where(diag, 16.0 * expand(27) + expand(28), 0.0)
        nrow = jnp.sum(index.reshape(sub // per, per, wide), axis=1).T
        for g in range(sub // per):
            column = jnp.broadcast_to(nrow[:, g:g + 1], (wide, 128))
            there = pl.ds(pl.multiple_of(r0 + g * per, per), per)
            lhs = lt[:, g * per:(g + 1) * per, :].reshape(27 * per, wide)
            for n in range(3):
                near = (column - float(n * halo)).astype(BF16)
                near = jnp.concatenate([near] * (halo // 128), axis=1)
                hot = jnp.where(near == b_lane, one, zero)
                res = jnp.dot(lhs, hot, preferred_element_type=F32).astype(BF16)
                res = res.reshape(9, 3, per, halo)
                for d in range(3):
                    mat[t, :, there, pl.ds(d * win + n * halo, halo)] = res[:, d]
        return carry

    units = atoms // sub
    first = units // 2
    lax.fori_loop(0, first, build, 0)
    for i in range(2):
        for p in range(1, nm):
            gather(p, i).wait_recv()
            edge(p, i).start()
    lax.fori_loop(first, units, build, 0)
    own_copy.wait()
    for p in range(1, nm):
        gather(p, 2).wait_recv()
    for i in range(2):
        for p in range(nm):
            edge(p, i).wait_recv()
    for copy in lcopies:
        copy.wait()

    def cross(x):
        return pltpu.make_async_remote_copy(
            src_ref=csend.at[x], dst_ref=crecv.at[x],
            send_sem=c_send.at[x], recv_sem=c_recv.at[x],
            device_id=at(m, sibling), device_id_type=MESH,
        )

    def along(x, s):
        return pltpu.make_async_remote_copy(
            src_ref=zsend.at[x, s - 1], dst_ref=zrecv.at[x, s - 1],
            send_sem=z_send.at[x, s - 1], recv_sem=z_recv.at[x, s - 1],
            device_id=at(m, lax.rem(a + 2 * s, na)), device_id_type=MESH,
        )

    def owner_rows(o):
        return pl.ds(pl.multiple_of(o * rows, 8), rows)

    def forward(x):
        cross(x).wait_recv()
        for s in [*range(1, nz), 0]:
            q = lax.rem(z + s, nz)
            both = cacc[x % 2, owner_rows(2 * q + core), :] + crecv[x, q, :rows, :].astype(F32)
            if s:
                zsend[x, s - 1, :rows, :] = both.astype(BF16)
                along(x, s).start()
            else:
                own[x] = both

    for x in range(3):
        def one_flux(i, carry, x=x):
            c, t = i // blocks, lax.rem(i, blocks)
            acc = jnp.zeros((panel, halo), F32)
            for d in range(3):
                acc += lax.dot_general(
                    rx[d, :, pl.ds(pl.multiple_of(t * halo, halo), win)],
                    mat[t, 3 * x + c, :, pl.ds(d * win, win)],
                    NT, preferred_element_type=F32,
                )
            flux[:, pl.ds(pl.multiple_of(i * halo, halo), halo)] = acc.astype(BF16)
            return carry

        mid = blocks
        lax.fori_loop(0, mid, one_flux, 0)
        if x:
            forward(x - 1)
        lax.fori_loop(mid, 3 * blocks, one_flux, 0)

        def one_coupling(n, carry, x=x):
            lanes = pl.ds(pl.multiple_of(n * 256, 256), 256)
            part = jnp.dot(flux[...], lv[:, lanes], preferred_element_type=F32)
            cacc[x % 2, lanes, :] = part.T
            return carry

        lax.fori_loop(0, nl // 256, one_coupling, 0)
        for q in range(nz):
            csend[x, q, :rows, :] = cacc[x % 2, owner_rows(2 * q + 1 - core), :].astype(BF16)
        cross(x).start()
    forward(2)

    squares = jnp.zeros((rows, panel), F32)
    for x in range(3):
        total = own[x]
        for s in range(1, nz):
            along(x, s).wait_recv()
            total += zrecv[x, s - 1, :rows, :].astype(F32)
        squares += total * total
    omega_left = omega_step * lbins[...].astype(F32)
    omega_right = omega_step * jnp.broadcast_to(rbins[...].astype(F32), (8, panel)).T[:, :1]
    gap = omega_left - omega_right
    weight = gamma * gamma / (gap * gap + gamma * gamma)
    both = omega_left + omega_right
    weight = weight * (both * both) / (4.0 * omega_left * omega_right)
    out[...] = 4.0 * jnp.sum(weight * squares.T, axis=0, keepdims=True) / (total_atoms * panel)

    for i in range(3):
        for p in range(1, nm):
            gather(p, i).wait_send()
    for i in range(2):
        for p in range(nm):
            edge(p, i).wait_send()
    for x in range(3):
        cross(x).wait_send()
        for s in range(1, nz):
            along(x, s).wait_send()


def per_device(
    nm, na,
    left_modes, right_panel, force_blocks, bond_vectors, neighbours, counts, left_bins, right_bins
):
    atoms, cols = right_panel.shape[1:]
    slots = neighbours.shape[0]
    nl = left_modes.shape[2]
    rows = left_bins.shape[0]
    panel = cols * nm
    halo = atoms // 4
    sub, wide = 128, 256
    nz = na // 2
    padded = -(-rows // 16) * 16
    vm = pl.BlockSpec(memory_space=pltpu.VMEM)
    hbm = pl.BlockSpec(memory_space=pl.ANY)
    dma = pltpu.SemaphoreType.DMA
    result = pl.pallas_call(
        functools.partial(kernel, nm, na),
        out_shape=jax.ShapeDtypeStruct((1, rows), F32),
        in_specs=[hbm, hbm, vm, vm, vm, vm, vm, vm],
        out_specs=vm,
        scratch_shapes=[
            pltpu.VMEM((3, panel, atoms + 2 * halo), BF16),
            pltpu.VMEM((3 * atoms, nl), BF16),
            pltpu.VMEM((atoms // halo, 9, halo, 9 * halo), BF16),
            pltpu.VMEM((27, sub, wide), BF16),
            pltpu.VMEM((panel, 3 * atoms), BF16),
            pltpu.VMEM((2, nl, panel), F32),
            pltpu.VMEM((3, nz, padded, panel), BF16),
            pltpu.VMEM((3, nz, padded, panel), BF16),
            pltpu.VMEM((3, nz - 1, padded, panel), BF16),
            pltpu.VMEM((3, nz - 1, padded, panel), BF16),
            pltpu.VMEM((3, rows, panel), F32),
            dma((nm - 1, 3)), dma((nm - 1, 3)),
            dma((nm, 2)), dma((nm, 2)),
            dma((3,)), dma((3,)),
            dma((3, nz - 1)), dma((3, nz - 1)),
            dma((3,)), dma,
        ],
        compiler_params=pltpu.CompilerParams(
            collective_id=0, has_side_effects=True, vmem_limit_bytes=60 * 2**20
        ),
    )(
        jnp.transpose(right_panel, (0, 2, 1)), left_modes,
        force_blocks.reshape(9, slots, atoms), bond_vectors, neighbours,
        counts[None, :], left_bins[None, :], right_bins[None, :],
    )
    return result.reshape(rows)


def solution(mesh):
    return jax.shard_map(
        functools.partial(per_device, mesh.shape["modes"], mesh.shape["atoms"]),
        mesh=mesh,
        in_specs=(
            P(None, "atoms", "modes"),
            P(None, "atoms", "modes"),
            P(None, None, None, "atoms"),
            P(None, None, "atoms"),
            P(None, "atoms"),
            P("atoms"),
            P(("modes", "atoms")),
            P(),
        ),
        out_specs=P(("modes", "atoms")),
        check_vma=False,
    )
```

```python
import functools

import jax
import jax.numpy as jnp
from jax import lax
from jax.experimental import pallas as pl
from jax.experimental.pallas import tpu as pltpu
from jax.sharding import PartitionSpec as P

omega_step = 0.05
gamma = 0.1
F32, BF16 = jnp.float32, jnp.bfloat16
MESH = pl.DeviceIdType.MESH
NT = (((1,), (1,)), ((), ()))


def kernel(
    nm, na,
    rt, left, force, bond, nbr, counts, lbins, rbins, out,
    rx, lv, mat, lt, flux, cacc, csend, crecv, zsend, zrecv, own,
    g_send, g_recv, h_send, h_recv, c_send, c_recv, z_send, z_recv, l_sem, o_sem,
):
    slots, atoms = nbr.shape
    cols = rt.shape[1]
    halo = atoms // 4
    blocks = atoms // halo
    win = 3 * halo
    sub = lt.shape[1]
    per = lt.shape[2] // slots
    wide = lt.shape[2]
    rows = lbins.shape[1]
    nz = na // 2
    panel = cols * nm
    nl = left.shape[2]
    total_atoms = atoms * na
    m = lax.axis_index("modes")
    a = lax.axis_index("atoms")
    core = lax.rem(a, 2)
    z = a // 2
    up, down = lax.rem(a + 1, na), lax.rem(a + na - 1, na)
    sibling = a + 1 - 2 * core

    def at(mode, atom):
        return {"modes": mode, "atoms": atom}

    barrier = pltpu.get_barrier_semaphore()
    friends = [at(lax.rem(m + p, nm), a) for p in range(1, nm)]
    friends += [at(m, up), at(m, down)]
    friends += [at(m, lax.rem(a + 2 * q, na)) for q in range(1, nz)]
    for friend in friends:
        pl.semaphore_signal(barrier, inc=1, device_id=friend, device_id_type=MESH)
    lcopies = [
        pltpu.make_async_copy(left.at[c], lv.at[pl.ds(c * atoms, atoms)], l_sem.at[c])
        for c in range(3)
    ]
    for copy in lcopies:
        copy.start()
    pl.semaphore_wait(barrier, len(friends))

    my_rows = pl.ds(pl.multiple_of(m * cols, cols), cols)
    pieces = ((0, halo), (atoms - halo, halo), (halo, atoms - 2 * halo))

    def gather(p, i):
        lane, count = pieces[i]
        return pltpu.make_async_remote_copy(
            src_ref=rt.at[:, :, pl.ds(lane, count)],
            dst_ref=rx.at[:, my_rows, pl.ds(halo + lane, count)],
            send_sem=g_send.at[p - 1, i],
            recv_sem=g_recv.at[p - 1, i],
            device_id=at(lax.rem(m + p, nm), a),
            device_id_type=MESH,
        )

    def edge(p, i):
        lane = pieces[i][0]
        who = lax.rem(m + nm - p, nm)
        its_rows = pl.ds(pl.multiple_of(who * cols, cols), cols)
        src = rt.at[:, :, pl.ds(lane, halo)] if p == 0 else rx.at[:, its_rows, pl.ds(halo + lane, halo)]
        return pltpu.make_async_remote_copy(
            src_ref=src,
            dst_ref=rx.at[:, its_rows, pl.ds(halo + atoms if i == 0 else 0, halo)],
            send_sem=h_send.at[p, i],
            recv_sem=h_recv.at[p, i],
            device_id=at(m, down if i == 0 else up),
            device_id_type=MESH,
        )

    own_copy = pltpu.make_async_copy(rt, rx.at[:, my_rows, pl.ds(halo, atoms)], o_sem)
    own_copy.start()
    for i in range(3):
        for p in range(1, nm):
            gather(p, i).start()
        if i < 2:
            edge(0, i).start()

    lane_id = lax.broadcasted_iota(jnp.int32, (sub, wide), 1)
    row_id = lax.broadcasted_iota(jnp.int32, (sub, wide), 0)
    diag = lax.rem(row_id, per) == lax.rem(lane_id, per)
    k_row = lax.broadcasted_iota(jnp.int32, (128, wide), 0)
    k_lane = lax.broadcasted_iota(jnp.int32, (128, wide), 1) // per
    groups_128 = 128 // slots
    b_lane = lax.broadcasted_iota(jnp.int32, (wide, halo), 1).astype(F32).astype(BF16)
    one, zero = jnp.ones((wide, halo), BF16), jnp.zeros((wide, halo), BF16)

    def build(u, carry):
        t = u // (halo // sub)
        r0 = lax.rem(u, halo // sub) * sub
        lanes = pl.ds(pl.multiple_of(u * sub, sub), sub)
        slot_ids = lax.broadcasted_iota(jnp.int32, (slots, sub), 0)
        live = (slot_ids < counts[:, lanes]).astype(F32)
        parts = []
        for x in range(3):
            scaled = bond[x, :, lanes] * live
            for cd in range(9):
                parts.append(scaled * force[cd, :, lanes])
        rel = nbr[:, lanes] - (a * atoms + t * halo - halo)
        rel = jnp.where(rel < 0, rel + total_atoms, rel)
        rel = jnp.where(rel >= total_atoms, rel - total_atoms, rel)
        parts.append((rel // 16).astype(F32))
        parts.append(lax.rem(rel, 16).astype(F32))
        while len(parts) % groups_128:
            parts.append(jnp.zeros((slots, sub), F32))
        spread = []
        for s in range(len(parts) // groups_128):
            block = jnp.concatenate(parts[s * groups_128:(s + 1) * groups_128], axis=0)
            spread.append(block.T.astype(BF16))

        def expand(i):
            chosen = (k_row == lax.rem(i, groups_128) * slots + k_lane).astype(F32).astype(BF16)
            return lax.dot_general(
                spread[i // groups_128], chosen, (((1,), (0,)), ((), ())),
                preferred_element_type=F32,
            )

        for i in range(27):
            lt[i] = jnp.where(diag, expand(i), 0.0).astype(BF16)
        index = jnp.where(diag, 16.0 * expand(27) + expand(28), 0.0)
        nrow = jnp.sum(index.reshape(sub // per, per, wide), axis=1).T
        for g in range(sub // per):
            column = jnp.broadcast_to(nrow[:, g:g + 1], (wide, 128))
            there = pl.ds(pl.multiple_of(r0 + g * per, per), per)
            lhs = lt[:, g * per:(g + 1) * per, :].reshape(27 * per, wide)
            for n in range(3):
                near = (column - float(n * halo)).astype(BF16)
                near = jnp.concatenate([near] * (halo // 128), axis=1)
                hot = jnp.where(near == b_lane, one, zero)
                res = jnp.dot(lhs, hot, preferred_element_type=F32).astype(BF16)
                res = res.reshape(9, 3, per, halo)
                for d in range(3):
                    mat[t, :, there, pl.ds(d * win + n * halo, halo)] = res[:, d]
        return carry

    units = atoms // sub
    first = units // 2
    lax.fori_loop(0, first, build, 0)
    for i in range(2):
        for p in range(1, nm):
            gather(p, i).wait_recv()
            edge(p, i).start()
    lax.fori_loop(first, units, build, 0)
    own_copy.wait()
    for p in range(1, nm):
        gather(p, 2).wait_recv()
    for i in range(2):
        for p in range(nm):
            edge(p, i).wait_recv()
    for copy in lcopies:
        copy.wait()

    def cross(x):
        return pltpu.make_async_remote_copy(
            src_ref=csend.at[x], dst_ref=crecv.at[x],
            send_sem=c_send.at[x], recv_sem=c_recv.at[x],
            device_id=at(m, sibling), device_id_type=MESH,
        )

    def along(x, s):
        return pltpu.make_async_remote_copy(
            src_ref=zsend.at[x, s - 1], dst_ref=zrecv.at[x, s - 1],
            send_sem=z_send.at[x, s - 1], recv_sem=z_recv.at[x, s - 1],
            device_id=at(m, lax.rem(a + 2 * s, na)), device_id_type=MESH,
        )

    def owner_rows(o):
        return pl.ds(pl.multiple_of(o * rows, 8), rows)

    def forward(x):
        cross(x).wait_recv()
        for s in [*range(1, nz), 0]:
            q = lax.rem(z + s, nz)
            both = cacc[x % 2, owner_rows(2 * q + core), :] + crecv[x, q, :rows, :].astype(F32)
            if s:
                zsend[x, s - 1, :rows, :] = both.astype(BF16)
                along(x, s).start()
            else:
                own[x] = both

    for x in range(3):
        def one_flux(i, carry, x=x):
            c, t = i // blocks, lax.rem(i, blocks)
            near = pl.ds(pl.multiple_of(t * halo, halo), win)
            lhs = jnp.concatenate([rx[d, :, near] for d in range(3)], axis=1)
            acc = lax.dot_general(lhs, mat[t, 3 * x + c], NT, preferred_element_type=F32)
            flux[:, pl.ds(pl.multiple_of(i * halo, halo), halo)] = acc.astype(BF16)
            return carry

        mid = blocks
        lax.fori_loop(0, mid, one_flux, 0, unroll=True)
        if x:
            forward(x - 1)
        lax.fori_loop(mid, 3 * blocks, one_flux, 0, unroll=True)

        def one_coupling(n, carry, x=x):
            lanes = pl.ds(pl.multiple_of(n * 256, 256), 256)
            part = jnp.dot(flux[...], lv[:, lanes], preferred_element_type=F32)
            cacc[x % 2, lanes, :] = part.T
            return carry

        lax.fori_loop(0, nl // 256, one_coupling, 0)
        for q in range(nz):
            csend[x, q, :rows, :] = cacc[x % 2, owner_rows(2 * q + 1 - core), :].astype(BF16)
        cross(x).start()
    forward(2)

    squares = jnp.zeros((rows, panel), F32)
    for x in range(3):
        total = own[x]
        for s in range(1, nz):
            along(x, s).wait_recv()
            total += zrecv[x, s - 1, :rows, :].astype(F32)
        squares += total * total
    omega_left = omega_step * lbins[...].astype(F32)
    omega_right = omega_step * jnp.broadcast_to(rbins[...].astype(F32), (8, panel)).T[:, :1]
    gap = omega_left - omega_right
    weight = gamma * gamma / (gap * gap + gamma * gamma)
    both = omega_left + omega_right
    weight = weight * (both * both) / (4.0 * omega_left * omega_right)
    out[...] = 4.0 * jnp.sum(weight * squares.T, axis=0, keepdims=True) / (total_atoms * panel)

    for i in range(3):
        for p in range(1, nm):
            gather(p, i).wait_send()
    for i in range(2):
        for p in range(nm):
            edge(p, i).wait_send()
    for x in range(3):
        cross(x).wait_send()
        for s in range(1, nz):
            along(x, s).wait_send()


def per_device(
    nm, na,
    left_modes, right_panel, force_blocks, bond_vectors, neighbours, counts, left_bins, right_bins
):
    atoms, cols = right_panel.shape[1:]
    slots = neighbours.shape[0]
    nl = left_modes.shape[2]
    rows = left_bins.shape[0]
    panel = cols * nm
    halo = atoms // 4
    sub, wide = 128, 256
    nz = na // 2
    padded = -(-rows // 16) * 16
    vm = pl.BlockSpec(memory_space=pltpu.VMEM)
    hbm = pl.BlockSpec(memory_space=pl.ANY)
    dma = pltpu.SemaphoreType.DMA
    result = pl.pallas_call(
        functools.partial(kernel, nm, na),
        out_shape=jax.ShapeDtypeStruct((1, rows), F32),
        in_specs=[hbm, hbm, vm, vm, vm, vm, vm, vm],
        out_specs=vm,
        scratch_shapes=[
            pltpu.VMEM((3, panel, atoms + 2 * halo), BF16),
            pltpu.VMEM((3 * atoms, nl), BF16),
            pltpu.VMEM((atoms // halo, 9, halo, 9 * halo), BF16),
            pltpu.VMEM((27, sub, wide), BF16),
            pltpu.VMEM((panel, 3 * atoms), BF16),
            pltpu.VMEM((2, nl, panel), F32),
            pltpu.VMEM((3, nz, padded, panel), BF16),
            pltpu.VMEM((3, nz, padded, panel), BF16),
            pltpu.VMEM((3, nz - 1, padded, panel), BF16),
            pltpu.VMEM((3, nz - 1, padded, panel), BF16),
            pltpu.VMEM((3, rows, panel), F32),
            dma((nm - 1, 3)), dma((nm - 1, 3)),
            dma((nm, 2)), dma((nm, 2)),
            dma((3,)), dma((3,)),
            dma((3, nz - 1)), dma((3, nz - 1)),
            dma((3,)), dma,
        ],
        compiler_params=pltpu.CompilerParams(
            collective_id=0, has_side_effects=True, vmem_limit_bytes=60 * 2**20
        ),
    )(
        jnp.transpose(right_panel, (0, 2, 1)), left_modes,
        force_blocks.reshape(9, slots, atoms), bond_vectors, neighbours,
        counts[None, :], left_bins[None, :], right_bins[None, :],
    )
    return result.reshape(rows)


def solution(mesh):
    return jax.shard_map(
        functools.partial(per_device, mesh.shape["modes"], mesh.shape["atoms"]),
        mesh=mesh,
        in_specs=(
            P(None, "atoms", "modes"),
            P(None, "atoms", "modes"),
            P(None, None, None, "atoms"),
            P(None, None, "atoms"),
            P(None, "atoms"),
            P("atoms"),
            P(("modes", "atoms")),
            P(),
        ),
        out_specs=P(("modes", "atoms")),
        check_vma=False,
    )
```
